128 devices in a mesh: dp: 2 (over z_hi), expert: 64 (over y, x, z_lo, core).
Axes of the slice: x: 4, y: 4, z: 4 (z_hi: 2, z_lo: 2; z = z_hi * 2 + z_lo), core: 2. Of those that a mesh axis runs over, the one named last changes fastest.
Arguments:
- tokens: bfloat16 [2048, 4096], P(('dp', 'expert')), may hold values from -6 to 6
- cotangent: bfloat16 [2048, 4096], P(('dp', 'expert')), may hold values from -6 to 6
- expert_ids: int32 [2048, 2], P(('dp', 'expert')), may hold values from 0 to 7, as said below
- gate_weights: float32 [2048, 2], P(('dp', 'expert')), may hold values from 0.2 to 1
- holder: int32 [8], replicated, may hold values from 0 to 7, as said below
- weight_in: bfloat16 [64, 4096, 256], P('expert'), may hold values from -6 to 6
- weight_out: bfloat16 [64, 128, 4096], P('expert'), may hold values from -6 to 6
- first_in: float32 [64, 4096, 256], P('expert', 'dp'), may hold values from -3 to 3
- second_in: float32 [64, 4096, 256], P('expert', 'dp'), may hold values from 0.1 to 1
- first_out: float32 [64, 128, 4096], P('expert', 'dp'), may hold values from -3 to 3
- second_out: float32 [64, 128, 4096], P('expert', 'dp'), may hold values from 0.1 to 1
Outputs:
- layer_out: bfloat16 [2048, 4096], P(('dp', 'expert'))
- grad_tokens: bfloat16 [2048, 4096], P(('dp', 'expert'))
- new_weight_in: bfloat16 [64, 4096, 256], P('expert', 'dp')
- new_weight_out: bfloat16 [64, 128, 4096], P('expert', 'dp')
- new_first_in: float32 [64, 4096, 256], P('expert', 'dp')
- new_second_in: float32 [64, 4096, 256], P('expert', 'dp')
- new_first_out: float32 [64, 128, 4096], P('expert', 'dp')
- new_second_out: float32 [64, 128, 4096], P('expert', 'dp')
The draws below stay inside these ranges and needn't reach their ends.
Inputs may be any that keep to these rules, and one draw needn't show every extreme that they name: `expert_ids`: each row names 2 different experts. No expert is named by more than 8 rows of one device, and on every device one expert is named by exactly 8 rows. A permutation: before the re-placement expert e holds slots e * 8 to e * 8 + 7, after it slots holder[e] * 8 onward; exactly 2 experts change place.
All inputs are finite; a program needn't handle non-finite values.
Results may differ from the reference program's by a relative error of at most 0.0064.
Values may be sent and summed in bfloat16 or wider, within the bound.
No kernel may reach another device: no remote copies, remote signals or barrier semaphores. Data moves between devices by JAX's collectives and lax.ppermute only.
A program may use at most 128 MiB of HBM per device.

```python
import math
import jax
import jax.numpy as jnp
from jax import lax

D = 4096
FF = 1024
EXPERTS = 8
TOPK = 2
MOVES = 2
TOK_DEV = 16
FFD = 128
SLOTS = 64
TOKENS = 2048
CAP = 8


def draw_expert_ids(key, part):
    key = jax.random.fold_in(key, 11)
    hottest = jax.random.randint(jax.random.fold_in(key, 1), (), 0, EXPERTS).astype(jnp.int32)
    routed = TOK_DEV * TOPK
    remain = routed - CAP
    others = jnp.arange(EXPERTS - 1, dtype=jnp.int32)
    others = others + (others >= hottest).astype(jnp.int32)
    candidates = jnp.repeat(others, CAP - 1)

    def one_block(block_key):
        first_key, second_key = jax.random.split(block_key)
        chosen = jnp.sort(jax.random.permutation(first_key, candidates)[:remain])
        listing = jnp.concatenate([jnp.full((CAP,), hottest, jnp.int32), chosen])
        layout = listing.reshape(TOPK, TOK_DEV).T
        return layout[jax.random.permutation(second_key, TOK_DEV)]
    block_keys = jax.random.split(jax.random.fold_in(key, 2), TOKENS // TOK_DEV)
    return jax.vmap(one_block)(block_keys).reshape(TOKENS, TOPK).astype(jnp.int32)


def draw_holder(key, part):
    key = jax.random.fold_in(key, 23)
    chosen = jax.random.permutation(key, EXPERTS)[:MOVES].astype(jnp.int32)
    rotated = jnp.roll(chosen, 1)
    return jnp.arange(EXPERTS, dtype=jnp.int32).at[chosen].set(rotated)


def shard_levels(stream_key, dims, pieces, low, high):
    gain, own = 1.0, jax.random.fold_in(stream_key, 6)
    for dim, blocks in pieces:
        draws = jnp.exp(jax.random.uniform(jax.random.fold_in(own, dim), (blocks,), jnp.float32, low / len(pieces), high / len(pieces)))
        gain = gain * jnp.repeat(draws, dims[dim] // blocks).reshape([-1 if axis == dim else 1 for axis in range(len(dims))])
    return gain


def bell_draw(key, shape, scale, bound, cuts=(), held_as=jnp.bfloat16):
    values = scale * jax.random.normal(key, shape, jnp.float32)
    if cuts:
        values = values * shard_levels(key, shape, cuts, -0.22, 0.18)
    return jnp.clip(values, -bound, bound).astype(held_as)


def setup_inputs(seed: int = 0) -> dict:
    key_of = jax.random.split(jax.random.key(seed), 12)
    return {
        "tokens": bell_draw(key_of[0], (TOKENS, D), 1.0, 6.0, ((0, 128),)),
        "cotangent": bell_draw(key_of[1], (TOKENS, D), 1.0, 6.0, ((0, 128),)),
        "expert_ids": draw_expert_ids(jax.random.fold_in(key_of[11], 71), 0),
        "gate_weights": jnp.clip(0.2 + 0.8 * jax.random.uniform(key_of[3], (TOKENS, TOPK), jnp.float32) ** shard_levels(key_of[3], (TOKENS, TOPK), ((0, 128),), -0.2, 0.2), 0.2, 1.0),
        "holder": draw_holder(jax.random.fold_in(key_of[11], 71), 0),
        "weight_in": bell_draw(key_of[5], (SLOTS, D, 2 * FFD), 1.0, 6.0, ((0, 64),)),
        "weight_out": bell_draw(key_of[6], (SLOTS, FFD, D), 1.0, 6.0, ((0, 64),)),
        "first_in": bell_draw(key_of[7], (SLOTS, D, 2 * FFD), 0.5, 3.0, ((0, 64), (1, 2)), jnp.float32),
        "second_in": jnp.clip(jnp.exp(math.log(1.0) - 2.3025851 * jax.random.uniform(key_of[8], (SLOTS, D, 2 * FFD), jnp.float32) ** shard_levels(key_of[8], (SLOTS, D, 2 * FFD), ((0, 64), (1, 2)), -0.2, 0.2)), 0.1, 1.0),
        "first_out": bell_draw(key_of[9], (SLOTS, FFD, D), 0.5, 3.0, ((0, 64), (1, 2)), jnp.float32),
        "second_out": jnp.clip(jnp.exp(math.log(1.0) - 2.3025851 * jax.random.uniform(key_of[10], (SLOTS, FFD, D), jnp.float32) ** shard_levels(key_of[10], (SLOTS, FFD, D), ((0, 64), (1, 2)), -0.2, 0.2)), 0.1, 1.0),
    }


beta_one = 0.9
beta_two = 0.95
learn_rate = 0.01
decay_rate = 0.1
epsilon = 1e-08
block_rows = 128

def forward_part(inputs, block_in, block_out):
    width = inputs.shape[1]
    hidden = block_out.shape[0]
    projected = jnp.dot(inputs, block_in, preferred_element_type=jnp.float32) * width ** (-0.5)
    gate_part = projected[:, :hidden]
    up_part = projected[:, hidden:]
    sigmoid = jax.nn.sigmoid(gate_part)
    activated = gate_part * sigmoid
    hidden_act = (activated * up_part).astype(jnp.bfloat16)
    outputs = (jnp.dot(hidden_act, block_out, preferred_element_type=jnp.float32) * FF ** (-0.5)).astype(jnp.bfloat16)
    return (outputs, (gate_part, up_part, sigmoid, activated, hidden_act))

def backward_part(inputs, cot_rows, kept_state, block_in, block_out):
    width = inputs.shape[1]
    gate_part, up_part, sigmoid, activated, hidden_act = kept_state
    grad_hidden = jnp.dot(cot_rows, block_out.T, preferred_element_type=jnp.float32) * FF ** (-0.5)
    slopes = sigmoid * (1.0 + gate_part * (1.0 - sigmoid))
    grad_gate = grad_hidden * up_part * slopes
    grad_up = grad_hidden * activated
    grad_pre = (jnp.concatenate([grad_gate, grad_up], axis=1) * width ** (-0.5)).astype(jnp.bfloat16)
    grad_rows = jnp.dot(grad_pre, block_in.T, preferred_element_type=jnp.float32).astype(jnp.bfloat16)
    grad_in = jnp.dot(inputs.T, grad_pre, preferred_element_type=jnp.float32)
    grad_out = jnp.dot(hidden_act.T, cot_rows, preferred_element_type=jnp.float32) * FF ** (-0.5)
    return (grad_rows, grad_in, grad_out)

def adam_step(weight, grad, first, second):
    first_new = beta_one * first + (1.0 - beta_one) * grad
    second_new = beta_two * second + (1.0 - beta_two) * grad * grad
    widened = weight.astype(jnp.float32)
    weight_new = (widened - learn_rate * (first_new / (jnp.sqrt(second_new) + epsilon) + decay_rate * widened)).astype(jnp.bfloat16)
    return (weight_new, first_new, second_new)

def reference(tokens, cotangent, expert_ids, gate_weights, holder, weight_in, weight_out, first_in, second_in, first_out, second_out):
    tok_total, width = tokens.shape
    top_count = expert_ids.shape[1]
    experts = holder.shape[0]
    slots = weight_in.shape[0]
    shards = slots // experts
    routed = tok_total * top_count
    flat_ids = expert_ids.reshape(routed).astype(jnp.int32)
    flat_gates = gate_weights.reshape(routed)
    counts = jnp.zeros((experts,), jnp.int32).at[flat_ids].add(1)
    starts = jnp.cumsum(counts) - counts
    padded = (counts + block_rows - 1) // block_rows * block_rows
    pad_ends = jnp.cumsum(padded).astype(jnp.int32)
    pad_starts = pad_ends - padded
    sort_order = jnp.argsort(flat_ids, stable=True).astype(jnp.int32)
    sorted_ids = flat_ids[sort_order]
    order_in = jnp.arange(routed, dtype=jnp.int32) - starts[sorted_ids]
    position = (pad_starts[sorted_ids] + order_in).astype(jnp.int32)
    blocks = (routed + block_rows - 1) // block_rows + experts
    row_table = jnp.full((blocks * block_rows,), routed, jnp.int32).at[position].set(sort_order)
    block_starts = jnp.arange(blocks, dtype=jnp.int32) * block_rows
    block_expert = jnp.minimum(lax.optimization_barrier(jnp.sum((pad_ends[None, :] <= block_starts[:, None]).astype(jnp.int32), axis=1)), experts - 1).astype(jnp.int32)
    shard_ids = jnp.arange(shards, dtype=jnp.int32)
    initial = (jnp.zeros((tok_total, width), jnp.float32), jnp.zeros((tok_total, width), jnp.float32), jnp.zeros(weight_in.shape, jnp.float32), jnp.zeros(weight_out.shape, jnp.float32))

    def block_step(totals, block_index):
        out_sum, grad_sum, grad_in_all, grad_out_all = totals
        row_ids = lax.dynamic_slice_in_dim(row_table, block_index * block_rows, block_rows)
        live_rows = row_ids < routed
        clipped = jnp.minimum(row_ids, routed - 1)
        token_of = clipped // top_count
        inputs = jnp.where(live_rows[:, None], tokens[token_of], jnp.zeros((), jnp.bfloat16))
        scaled = (flat_gates[clipped][:, None] * cotangent[token_of].astype(jnp.float32)).astype(jnp.bfloat16)
        cot_rows = jnp.where(live_rows[:, None], scaled, jnp.zeros((), jnp.bfloat16))
        expert = block_expert[block_index]

        def shard_step(carry, shard):
            out_acc, grad_acc = carry
            slot = expert * shards + shard
            block_in = weight_in[slot]
            block_out = weight_out[slot]
            outputs, kept_state = forward_part(inputs, block_in, block_out)
            grad_rows, part_in, part_out = backward_part(inputs, cot_rows, kept_state, block_in, block_out)
            return ((out_acc + outputs.astype(jnp.float32), grad_acc + grad_rows.astype(jnp.float32)), (part_in, part_out))
        start = (jnp.zeros((block_rows, width), jnp.float32), jnp.zeros((block_rows, width), jnp.float32))
        sums, parts = lax.scan(shard_step, start, shard_ids)
        gate_here = jnp.where(live_rows, flat_gates[clipped], jnp.zeros((), jnp.float32))
        out_sum = out_sum.at[token_of].add(gate_here[:, None] * sums[0])
        grad_sum = grad_sum.at[token_of].add(jnp.where(live_rows[:, None], sums[1], jnp.zeros((), jnp.float32)))
        slot_list = (expert * shards + shard_ids).astype(jnp.int32)
        grad_in_all = grad_in_all.at[slot_list].add(parts[0])
        grad_out_all = grad_out_all.at[slot_list].add(parts[1])
        return ((out_sum, grad_sum, grad_in_all, grad_out_all), None)
    totals, _ = lax.scan(block_step, initial, jnp.arange(blocks, dtype=jnp.int32))
    out_sum, grad_sum, grad_in_all, grad_out_all = totals
    anchor = jnp.zeros((experts,), jnp.int32).at[holder].set(jnp.arange(experts, dtype=jnp.int32))
    slot_ids = jnp.arange(slots, dtype=jnp.int32)
    slot_from = (anchor[slot_ids // shards] * shards + slot_ids % shards).astype(jnp.int32)
    new_weight_in, new_first_in, new_second_in = adam_step(weight_in[slot_from], grad_in_all[slot_from], first_in[slot_from], second_in[slot_from])
    new_weight_out, new_first_out, new_second_out = adam_step(weight_out[slot_from], grad_out_all[slot_from], first_out[slot_from], second_out[slot_from])
    return (out_sum.astype(jnp.bfloat16), grad_sum.astype(jnp.bfloat16), new_weight_in, new_weight_out, new_first_in, new_second_in, new_first_out, new_second_out)
```

```python
import jax
import jax.numpy as jnp
from jax import lax
from jax.sharding import Mesh, PartitionSpec as P

FF = 1024

beta_one = 0.9
beta_two = 0.95
learn_rate = 0.01
decay_rate = 0.1
epsilon = 1e-08

PARTS = ("y", "xh", "xl", "z", "c")
GROUP = ("y", "xh")
FLIP = [(0, 1), (1, 0)]
half_type = jnp.bfloat16


def adam_step(weight, grad, first, second):
    first_new = beta_one * first + (1.0 - beta_one) * grad
    second_new = beta_two * second + (1.0 - beta_two) * grad * grad
    widened = weight.astype(jnp.float32)
    weight_new = (
        widened - learn_rate * (first_new / (jnp.sqrt(second_new) + epsilon) + decay_rate * widened)
    ).astype(jnp.bfloat16)
    return (weight_new, first_new, second_new)


def flip(value, axis):
    return lax.ppermute(value, axis, FLIP)


def gather_group(piece):
    rows = piece.shape[0] // 2
    from_x = flip(piece, "xl")
    from_z = flip(piece, "z")
    diag = jnp.concatenate([flip(from_z[:rows], "xl"), flip(from_x[rows:], "z")], axis=0)
    mine = jnp.stack([piece, from_x, from_z, diag])
    other = flip(mine, "c")
    return mine, other


def reduce_group(mine, other):
    rows = mine.shape[1] // 2
    wide = mine.astype(jnp.float32) + flip(other, "c").astype(jnp.float32)
    own, to_x, to_z, diag = wide[0], wide[1], wide[2], wide[3].astype(half_type)
    via_x = flip(diag[:rows], "xl").astype(jnp.float32)
    via_z = flip(diag[rows:], "z").astype(jnp.float32)
    to_z = jnp.concatenate([to_z[:rows] + via_x, to_z[rows:]], axis=0).astype(half_type)
    to_x = jnp.concatenate([to_x[:rows], to_x[rows:] + via_z], axis=0).astype(half_type)
    return own + flip(to_x, "xl").astype(jnp.float32) + flip(to_z, "z").astype(jnp.float32)


def swap_branches(experts, shards):
    def one(low, high):
        pairs = []
        for shard in range(shards):
            pairs.append((low * shards + shard, high * shards + shard))
            pairs.append((high * shards + shard, low * shards + shard))

        def move(values):
            return tuple(lax.ppermute(value, PARTS, pairs) for value in values)

        return move

    return [one(low, high) for low in range(experts) for high in range(low + 1, experts)]


def on_device(
    tokens,
    cotangent,
    expert_ids,
    gate_weights,
    holder,
    weight_in,
    weight_out,
    first_in,
    second_in,
    first_out,
    second_out,
):
    tok_rows, width = tokens.shape
    top_count = expert_ids.shape[1]
    groups = holder.shape[0]
    shards = 8
    routed = tok_rows * top_count
    capacity = 2 * routed // groups
    hidden = weight_out.shape[1]
    data_half = lax.axis_index("dp")
    columns = jnp.arange(groups, dtype=jnp.int32)
    my_expert = lax.axis_index("y") * 2 + lax.axis_index("xh")
    changed = holder != columns
    low = jnp.min(jnp.where(changed, columns, groups - 1))
    high = jnp.max(jnp.where(changed, columns, 0))
    case = low * (2 * groups - 1 - low) // 2 + (high - low - 1)
    branches = swap_branches(groups, shards)
    case = jnp.clip(case, 0, len(branches) - 1)
    moved = (my_expert == low) | (my_expert == high)
    slot_in = weight_in[0]
    slot_out = weight_out[0]
    states = (first_in[0], second_in[0], first_out[0], second_out[0])
    rows_in_half = first_in.shape[1]
    rows_out_half = first_out.shape[1]
    half_w_in = lax.dynamic_slice_in_dim(slot_in, data_half * rows_in_half, rows_in_half, 0)
    half_w_out = lax.dynamic_slice_in_dim(slot_out, data_half * rows_out_half, rows_out_half, 0)

    flat_ids = expert_ids.reshape(routed)
    onehot = (flat_ids[:, None] == columns[None, :]).astype(jnp.int32)
    earlier = jnp.cumsum(onehot, axis=0) - onehot
    order_in = jnp.sum(earlier * onehot, axis=1)
    position = (flat_ids * capacity + order_in).reshape(tok_rows, top_count)
    places = jnp.arange(groups * capacity, dtype=jnp.int32)
    picks = position[:, :, None] == places[None, None, :]
    chosen = jnp.any(picks, axis=1).astype(jnp.bfloat16)
    gate_of = jnp.sum(jnp.where(picks, gate_weights[:, :, None], 0.0), axis=(0, 1))
    spread = (((0,), (0,)), ((), ()))
    group_inputs = lax.dot_general(chosen, tokens, spread, preferred_element_type=jnp.float32).astype(jnp.bfloat16)
    group_cots = (
        gate_of[:, None] * lax.dot_general(chosen, cotangent, spread, preferred_element_type=jnp.float32)
    ).astype(jnp.bfloat16)
    send = jnp.concatenate(
        [group_inputs.reshape(groups, capacity, width), group_cots.reshape(groups, capacity, width)], axis=1
    )
    received = lax.all_to_all(send, GROUP, split_axis=0, concat_axis=0, tiled=True)
    rows_piece = received[:, :capacity].reshape(groups * capacity, width)
    cots_piece = received[:, capacity:].reshape(groups * capacity, width)
    in_mine, in_other = gather_group(rows_piece)
    cot_mine, cot_other = gather_group(cots_piece)
    rows_in = jnp.concatenate([in_mine, in_other]).reshape(-1, width)
    rows_cot = jnp.concatenate([cot_mine, cot_other]).reshape(-1, width)

    early = lax.switch(
        case,
        branches,
        (
            states[0].astype(half_type),
            states[1].astype(half_type),
            states[2].astype(half_type),
            states[3].astype(half_type),
            half_w_in,
            half_w_out,
        ),
    )

    last_dims = (((1,), (1,)), ((), ()))
    first_dims = (((0,), (0,)), ((), ()))
    projected = jnp.dot(rows_in, slot_in, preferred_element_type=jnp.float32) * width ** (-0.5)
    gate_part = projected[:, :hidden]
    up_part = projected[:, hidden:]
    sigmoid = jax.nn.sigmoid(gate_part)
    activated = gate_part * sigmoid
    hidden_act = (activated * up_part).astype(jnp.bfloat16)
    outputs = (jnp.dot(hidden_act, slot_out, preferred_element_type=jnp.float32) * FF ** (-0.5)).astype(jnp.bfloat16)
    grad_hidden = lax.dot_general(rows_cot, slot_out, last_dims, preferred_element_type=jnp.float32) * FF ** (-0.5)
    slopes = sigmoid * (1.0 + gate_part * (1.0 - sigmoid))
    grad_gate = grad_hidden * up_part * slopes
    grad_up = grad_hidden * activated
    grad_pre = (jnp.concatenate([grad_gate, grad_up], axis=1) * width ** (-0.5)).astype(jnp.bfloat16)
    grad_rows = lax.dot_general(grad_pre, slot_in, last_dims, preferred_element_type=jnp.float32).astype(jnp.bfloat16)
    grad_in = lax.dot_general(rows_in, grad_pre, first_dims, preferred_element_type=jnp.float32)
    grad_out = lax.dot_general(hidden_act, rows_cot, first_dims, preferred_element_type=jnp.float32) * FF ** (-0.5)

    other_half = 1 - data_half
    away_in = lax.dynamic_slice_in_dim(grad_in, other_half * rows_in_half, rows_in_half, 0).astype(half_type)
    away_out = lax.dynamic_slice_in_dim(grad_out, other_half * rows_out_half, rows_out_half, 0).astype(half_type)
    half_in = lax.dynamic_slice_in_dim(grad_in, data_half * rows_in_half, rows_in_half, 0) + flip(away_in, "dp").astype(jnp.float32)
    half_out = lax.dynamic_slice_in_dim(grad_out, data_half * rows_out_half, rows_out_half, 0) + flip(away_out, "dp").astype(jnp.float32)
    late = lax.switch(case, branches, (half_in.astype(half_type), half_out.astype(half_type)))

    out_pieces = outputs.reshape(2, 4, groups * capacity, width)
    grad_pieces = grad_rows.reshape(2, 4, groups * capacity, width)
    out_sum = reduce_group(out_pieces[0], out_pieces[1])
    grad_sum = reduce_group(grad_pieces[0], grad_pieces[1])
    back = jnp.concatenate(
        [
            out_sum.astype(half_type).reshape(groups, capacity, width),
            grad_sum.astype(half_type).reshape(groups, capacity, width),
        ],
        axis=1,
    )
    back = lax.all_to_all(back, GROUP, split_axis=0, concat_axis=0, tiled=True)
    back_out = back[:, :capacity].reshape(groups * capacity, width)
    back_grad = back[:, capacity:].reshape(groups * capacity, width)
    picked = picks.astype(jnp.bfloat16)
    layer_out = sum(
        gate_weights[:, k : k + 1] * jnp.dot(picked[:, k], back_out, preferred_element_type=jnp.float32)
        for k in range(top_count)
    ).astype(jnp.bfloat16)
    grad_tokens = jnp.dot(chosen, back_grad, preferred_element_type=jnp.float32).astype(jnp.bfloat16)

    def placed(came, stayed):
        return jnp.where(moved, came.astype(stayed.dtype), stayed)

    new_weight_in, new_first_in, new_second_in = adam_step(
        placed(early[4], half_w_in), placed(late[0], half_in), placed(early[0], states[0]), placed(early[1], states[1])
    )
    new_weight_out, new_first_out, new_second_out = adam_step(
        placed(early[5], half_w_out), placed(late[1], half_out), placed(early[2], states[2]), placed(early[3], states[3])
    )
    return (
        layer_out,
        grad_tokens,
        new_weight_in[None],
        new_weight_out[None],
        new_first_in[None],
        new_second_in[None],
        new_first_out[None],
        new_second_out[None],
    )


def solution(mesh):
    fine = Mesh(mesh.devices.reshape(2, 4, 2, 2, 2, 2), ("dp",) + PARTS)
    rows = P(("dp",) + PARTS, None)
    slots = P(PARTS, None, None)
    halves = P(PARTS, "dp", None)
    return jax.shard_map(
        on_device,
        mesh=fine,
        in_specs=(rows, rows, rows, rows, P(), slots, slots, halves, halves, halves, halves),
        out_specs=(rows, rows, halves, halves, halves, halves, halves, halves),
        check_vma=False,
    )
```

```python
import functools

import jax
import jax.numpy as jnp
from jax import lax
from jax.experimental import pallas as pl
from jax.experimental.pallas import tpu as pltpu
from jax.sharding import Mesh, PartitionSpec as P

FF = 1024

beta_one = 0.9
beta_two = 0.95
learn_rate = 0.01
decay_rate = 0.1
epsilon = 1e-08

PARTS = ("y", "xh", "xl", "z", "c")
GROUP = ("y", "xh")
DISTANCES = range(1, 8)
FLIP = [(0, 1), (1, 0)]
half_type = jnp.bfloat16


def adam_step(weight, grad, first, second):
    first_new = beta_one * first + (1.0 - beta_one) * grad
    second_new = beta_two * second + (1.0 - beta_two) * grad * grad
    weight_new = (
        weight - learn_rate * (first_new / (jnp.sqrt(second_new) + epsilon) + decay_rate * weight)
    ).astype(jnp.bfloat16)
    return (weight_new, first_new, second_new)


STEPS = 8


def sections(inner_rows, outer_rows, lanes, outer_columns):
    parts = outer_columns // lanes
    inner = [slice(k * inner_rows, (k + 1) * inner_rows) for k in range(3)]
    start = 3 * inner_rows
    outer = [
        [
            slice(start + (k * parts + p) * outer_rows, start + (k * parts + p + 1) * outer_rows)
            for p in range(parts)
        ]
        for k in range(3)
    ]
    return inner, outer


def step_specs(inner, outer):
    rows, lanes = inner.shape[0] // STEPS, inner.shape[1]
    outer_rows, columns = outer.shape[0], outer.shape[1] // STEPS
    inner_spec = pl.BlockSpec((rows, lanes), lambda i, at: (i, 0))
    outer_spec = pl.BlockSpec((outer_rows, columns), lambda i, at: (0, i))
    whole_inner = pl.BlockSpec((rows, lanes), lambda i, at: (at[0] * STEPS + i, 0))
    whole_outer = pl.BlockSpec((outer_rows, columns), lambda i, at: (at[0], i))
    height = 3 * rows + 3 * outer_rows * columns // lanes
    packed_spec = pl.BlockSpec((1, height, lanes), lambda i, at: (i, 0, 0))
    return inner_spec, outer_spec, whole_inner, whole_outer, packed_spec


def pack_kernel(at, first_in, second_in, weight_in, first_out, second_out, weight_out, packed):
    lanes = first_in.shape[1]
    inner, outer = sections(first_in.shape[0], first_out.shape[0], lanes, first_out.shape[1])
    moved = at[1] == 1

    def put(rows, value):
        packed[0, rows, :] = jnp.where(moved, value.astype(jnp.float32), 0.0).astype(packed.dtype)

    for rows, ref in zip(inner, (first_in, second_in, weight_in)):
        put(rows, ref[...])
    for parts, ref in zip(outer, (first_out, second_out, weight_out)):
        for p, rows in enumerate(parts):
            put(rows, ref[:, p * lanes : (p + 1) * lanes])


def pack(at, states, slot_in, slot_out):
    inner_spec, outer_spec, whole_inner, whole_outer, packed_spec = step_specs(states[0], states[2])
    return pl.pallas_call(
        pack_kernel,
        grid_spec=pltpu.PrefetchScalarGridSpec(
            num_scalar_prefetch=1,
            grid=(STEPS,),
            in_specs=[inner_spec, inner_spec, whole_inner, outer_spec, outer_spec, whole_outer],
            out_specs=packed_spec,
        ),
        out_shape=jax.ShapeDtypeStruct((STEPS,) + packed_spec.block_shape[1:], half_type),
        cost_estimate=pl.CostEstimate(flops=4 << 20, bytes_accessed=24 << 20, transcendentals=0),
    )(at, states[0], states[1], slot_in, states[2], states[3], slot_out)


def adam_kernel(
    at,
    packed,
    first_in,
    second_in,
    weight_in,
    first_out,
    second_out,
    weight_out,
    grad_in,
    grad_out,
    late_in,
    late_out,
    new_weight_in,
    new_first_in,
    new_second_in,
    new_weight_out,
    new_first_out,
    new_second_out,
):
    lanes = first_in.shape[1]
    inner, outer = sections(first_in.shape[0], first_out.shape[0], lanes, first_out.shape[1])
    moved = at[1] == 1

    def placed(rows, stayed):
        came = packed[0, rows, :].astype(jnp.float32) - stayed.astype(half_type).astype(jnp.float32)
        return jnp.where(moved, came, stayed.astype(jnp.float32))

    new_weight_in[...], new_first_in[...], new_second_in[...] = adam_step(
        placed(inner[2], weight_in[...]),
        jnp.where(moved, late_in[...].astype(jnp.float32), grad_in[...]),
        placed(inner[0], first_in[...]),
        placed(inner[1], second_in[...]),
    )
    for p in range(len(outer[0])):
        part = slice(p * lanes, (p + 1) * lanes)
        new_weight_out[:, part], new_first_out[:, part], new_second_out[:, part] = adam_step(
            placed(outer[2][p], weight_out[:, part]),
            jnp.where(moved, late_out[:, part].astype(jnp.float32), grad_out[:, part]),
            placed(outer[0][p], first_out[:, part]),
            placed(outer[1][p], second_out[:, part]),
        )


def adam(at, packed, states, slot_in, slot_out, grad_in, grad_out, late_in, late_out):
    inner_spec, outer_spec, whole_inner, whole_outer, packed_spec = step_specs(states[0], states[2])
    inner_shape, outer_shape = states[0].shape, states[2].shape
    return pl.pallas_call(
        adam_kernel,
        grid_spec=pltpu.PrefetchScalarGridSpec(
            num_scalar_prefetch=1,
            grid=(STEPS,),
            in_specs=[packed_spec, inner_spec, inner_spec, whole_inner, outer_spec, outer_spec, whole_outer]
            + [inner_spec, outer_spec, inner_spec, outer_spec],
            out_specs=[inner_spec] * 3 + [outer_spec] * 3,
        ),
        out_shape=[
            jax.ShapeDtypeStruct(shape, dtype)
            for shape in (inner_shape, outer_shape)
            for dtype in (jnp.bfloat16, jnp.float32, jnp.float32)
        ],
        cost_estimate=pl.CostEstimate(flops=16 << 20, bytes_accessed=30 << 20, transcendentals=1 << 20),
        compiler_params=pltpu.CompilerParams(vmem_limit_bytes=24 * 1024 * 1024),
    )(at, packed, states[0], states[1], slot_in, states[2], states[3], slot_out, grad_in, grad_out, late_in, late_out)


def flip(value, axis):
    return lax.ppermute(value, axis, FLIP)


def tie(first, *others):
    return lax.optimization_barrier((first,) + others)[0]


def split_at(rows, share):
    return int(rows * share) // 16 * 16


def gather_groups(pieces, share, holds):
    cut = split_at(pieces[0].shape[0], share)
    near = [(flip(piece, "xl"), flip(piece, "z"), flip(piece, "c")) for piece in pieces]
    gathered = []
    last = None
    for piece, (from_x, from_z, from_c), hold in zip(pieces, near, holds):
        if last is not None:
            from_x, from_z = tie((from_x, from_z), last)
        if hold is not None:
            from_x, from_z = tie((from_x, from_z), hold)
        parts = []
        if cut:
            parts.append(flip(from_z[:cut], "xl"))
        if cut < piece.shape[0]:
            parts.append(flip(from_x[cut:], "z"))
        sides = flip(jnp.concatenate([from_x, from_z]), "c")
        diag = jnp.concatenate(parts)
        gathered.append([piece, from_x, from_z, from_c, sides, diag, flip(diag, "c")])
        last = diag
    return [jnp.concatenate(parts) for parts in gathered]


def reduce_start(array, share):
    rows = array.shape[0] // 8
    piece = lambda start, count=1: array[start * rows : (start + count) * rows]
    cut = split_at(rows, share)
    diag = (piece(6).astype(jnp.float32) + flip(piece(7), "c").astype(jnp.float32)).astype(half_type)
    sides = piece(1, 2).astype(jnp.float32) + flip(piece(4, 2), "c").astype(jnp.float32)
    own = piece(0).astype(jnp.float32) + flip(piece(3), "c").astype(jnp.float32)
    to_x, to_z = sides[:rows], sides[rows:]
    if cut:
        via_x = flip(diag[:cut], "xl").astype(jnp.float32)
        to_z = jnp.concatenate([to_z[:cut] + via_x, to_z[cut:]])
    if cut < rows:
        via_z = flip(diag[cut:], "z").astype(jnp.float32)
        to_x = jnp.concatenate([to_x[:cut], to_x[cut:] + via_z])
    return own, to_x.astype(half_type), to_z.astype(half_type)


def exchange(values, distance):
    pairs = [(slot, slot ^ (distance * 8)) for slot in range(64)]
    return tuple(lax.ppermute(value, PARTS, pairs) for value in values)


def late_steps(values, rows_to_x, rows_to_z, distance):
    moved = exchange(values, distance)
    return moved, tuple(flip(rows, "xl") for rows in rows_to_x), tuple(flip(rows, "z") for rows in rows_to_z)


def on_device(
    tokens,
    cotangent,
    expert_ids,
    gate_weights,
    holder,
    weight_in,
    weight_out,
    first_in,
    second_in,
    first_out,
    second_out,
):
    tok_rows, width = tokens.shape
    top_count = expert_ids.shape[1]
    groups = holder.shape[0]
    shards = 8
    routed = tok_rows * top_count
    capacity = 2 * routed // groups
    hidden = weight_out.shape[1]
    data_half = lax.axis_index("dp")
    columns = jnp.arange(groups, dtype=jnp.int32)
    my_expert = lax.axis_index("y") * 2 + lax.axis_index("xh")
    changed = holder != columns
    low = jnp.min(jnp.where(changed, columns, groups - 1))
    high = jnp.max(jnp.where(changed, columns, 0))
    case = jnp.clip((low ^ high) - 1, 0, 6)
    moved = (my_expert == low) | (my_expert == high)
    slot_in = weight_in[0]
    slot_out = weight_out[0]
    states = (first_in[0], second_in[0], first_out[0], second_out[0])
    rows_in_half = first_in.shape[1]
    rows_out_half = first_out.shape[1]
    at = jnp.stack([data_half, moved]).astype(jnp.int32)

    flat_ids = expert_ids.reshape(routed)
    onehot = (flat_ids[:, None] == columns[None, :]).astype(jnp.int32)
    earlier = jnp.cumsum(onehot, axis=0) - onehot
    order_in = jnp.sum(earlier * onehot, axis=1)
    position = (flat_ids * capacity + order_in).reshape(tok_rows, top_count)
    places = jnp.arange(groups * capacity, dtype=jnp.int32)
    picks = position[:, :, None] == places[None, None, :]
    chosen = jnp.any(picks, axis=1).astype(jnp.bfloat16)
    gate_of = jnp.sum(jnp.where(picks, gate_weights[:, :, None], 0.0), axis=(0, 1))
    spread = (((0,), (0,)), ((), ()))
    group_inputs = lax.dot_general(chosen, tokens, spread, preferred_element_type=jnp.float32).astype(jnp.bfloat16)
    group_cots = (
        gate_of[:, None] * lax.dot_general(chosen, cotangent, spread, preferred_element_type=jnp.float32)
    ).astype(jnp.bfloat16)
    send = jnp.concatenate(
        [group_inputs.reshape(groups, capacity, width), group_cots.reshape(groups, capacity, width)], axis=1
    )
    at, send = lax.optimization_barrier((at, send))
    share = lax.psum_scatter(pack(at, states, slot_in, slot_out), GROUP, scatter_dimension=0, tiled=True)
    received = lax.all_to_all(send, GROUP, split_axis=0, concat_axis=0, tiled=True)
    rows_piece = received[:, :capacity].reshape(groups * capacity, width)
    cots_piece = received[:, capacity:].reshape(groups * capacity, width)
    rows_in, rows_cot = gather_groups((rows_piece, cots_piece), 0.5, (None, None))

    last_dims = (((1,), (1,)), ((), ()))
    first_dims = (((0,), (0,)), ((), ()))
    projected = jnp.dot(rows_in, slot_in, preferred_element_type=jnp.float32) * width ** (-0.5)
    gate_part = projected[:, :hidden]
    up_part = projected[:, hidden:]
    sigmoid = jax.nn.sigmoid(gate_part)
    activated = gate_part * sigmoid
    hidden_act = (activated * up_part).astype(jnp.bfloat16)
    outputs = (jnp.dot(hidden_act, slot_out, preferred_element_type=jnp.float32) * FF ** (-0.5)).astype(jnp.bfloat16)
    grad_hidden = lax.dot_general(rows_cot, slot_out, last_dims, preferred_element_type=jnp.float32) * FF ** (-0.5)
    slopes = sigmoid * (1.0 + gate_part * (1.0 - sigmoid))
    grad_gate = grad_hidden * up_part * slopes
    grad_up = grad_hidden * activated
    grad_pre = (jnp.concatenate([grad_gate, grad_up], axis=1) * width ** (-0.5)).astype(jnp.bfloat16)
    grad_rows = lax.dot_general(grad_pre, slot_in, last_dims, preferred_element_type=jnp.float32).astype(jnp.bfloat16)
    grad_in = lax.dot_general(rows_in, grad_pre, first_dims, preferred_element_type=jnp.float32)
    grad_out = lax.dot_general(hidden_act, rows_cot, first_dims, preferred_element_type=jnp.float32) * FF ** (-0.5)

    other_half = 1 - data_half
    away_in = lax.dynamic_slice_in_dim(grad_in, other_half * rows_in_half, rows_in_half, 0).astype(half_type)
    away_out = lax.dynamic_slice_in_dim(grad_out, other_half * rows_out_half, rows_out_half, 0).astype(half_type)
    kept_in = lax.dynamic_slice_in_dim(grad_in, data_half * rows_in_half, rows_in_half, 0)
    kept_out = lax.dynamic_slice_in_dim(grad_out, data_half * rows_out_half, rows_out_half, 0)
    came_out = flip(away_out, "dp")
    half_out = kept_out + came_out.astype(jnp.float32)
    half_in = kept_in + flip(away_in, "dp").astype(jnp.float32)
    half_in, half_out, share = lax.optimization_barrier((half_in, half_out, share))
    early = lax.all_gather(share, GROUP, axis=0, tiled=True)

    own_out, out_to_x, out_to_z = reduce_start(outputs, 0.5)
    own_grad, grad_to_x, grad_to_z = reduce_start(grad_rows, 0.5)
    (late_in, late_out), from_x, from_z = lax.switch(
        case,
        [functools.partial(late_steps, distance=distance) for distance in DISTANCES],
        (half_in.astype(half_type), half_out.astype(half_type)),
        (out_to_x, grad_to_x),
        (out_to_z, grad_to_z),
    )
    out_sum, grad_sum = (
        own + part_x.astype(jnp.float32) + part_z.astype(jnp.float32)
        for own, part_x, part_z in zip((own_out, own_grad), from_x, from_z)
    )
    back = jnp.concatenate(
        [
            out_sum.astype(half_type).reshape(groups, capacity, width),
            grad_sum.astype(half_type).reshape(groups, capacity, width),
        ],
        axis=1,
    )
    back = lax.all_to_all(back, GROUP, split_axis=0, concat_axis=0, tiled=True)
    new_weight_in, new_first_in, new_second_in, new_weight_out, new_first_out, new_second_out = adam(
        at, early, states, slot_in, slot_out, half_in, half_out, late_in, late_out
    )
    back, new_weight_in = lax.optimization_barrier((back, new_weight_in))
    back_out = back[:, :capacity].reshape(groups * capacity, width)
    back_grad = back[:, capacity:].reshape(groups * capacity, width)
    picked = picks.astype(jnp.bfloat16)
    layer_out = sum(
        gate_weights[:, k : k + 1] * jnp.dot(picked[:, k], back_out, preferred_element_type=jnp.float32)
        for k in range(top_count)
    ).astype(jnp.bfloat16)
    grad_tokens = jnp.dot(chosen, back_grad, preferred_element_type=jnp.float32).astype(jnp.bfloat16)

    return (
        layer_out,
        grad_tokens,
        new_weight_in[None],
        new_weight_out[None],
        new_first_in[None],
        new_second_in[None],
        new_first_out[None],
        new_second_out[None],
    )


def solution(mesh):
    fine = Mesh(mesh.devices.reshape(2, 4, 2, 2, 2, 2), ("dp",) + PARTS)
    rows = P(("dp",) + PARTS, None)
    slots = P(PARTS, None, None)
    halves = P(PARTS, "dp", None)
    return jax.shard_map(
        on_device,
        mesh=fine,
        in_specs=(rows, rows, rows, rows, P(), slots, slots, halves, halves, halves, halves),
        out_specs=(rows, rows, halves, halves, halves, halves, halves, halves),
        check_vma=False,
    )
```

```python
import functools

import jax
import jax.numpy as jnp
from jax import lax
from jax.experimental import pallas as pl
from jax.experimental.pallas import tpu as pltpu
from jax.sharding import Mesh, PartitionSpec as P

FF = 1024

beta_one = 0.9
beta_two = 0.95
learn_rate = 0.01
decay_rate = 0.1
epsilon = 1e-08

PARTS = ("y", "xh", "xl", "z", "c")
GROUP = ("y", "xh")
DISTANCES = range(1, 8)
FLIP = [(0, 1), (1, 0)]
half_type = jnp.bfloat16


def adam_step(weight, grad, first, second):
    first_new = beta_one * first + (1.0 - beta_one) * grad
    second_new = beta_two * second + (1.0 - beta_two) * grad * grad
    weight_new = (
        weight - learn_rate * (first_new / (jnp.sqrt(second_new) + epsilon) + decay_rate * weight)
    ).astype(jnp.bfloat16)
    return (weight_new, first_new, second_new)


STEPS = 8


def sections(inner_rows, outer_rows, lanes, outer_columns):
    parts = outer_columns // lanes
    inner = [slice(k * inner_rows, (k + 1) * inner_rows) for k in range(3)]
    start = 3 * inner_rows
    outer = [
        [
            slice(start + (k * parts + p) * outer_rows, start + (k * parts + p + 1) * outer_rows)
            for p in range(parts)
        ]
        for k in range(3)
    ]
    return inner, outer


def step_specs(inner, outer):
    rows, lanes = inner.shape[0] // STEPS, inner.shape[1]
    outer_rows, columns = outer.shape[0], outer.shape[1] // STEPS
    inner_spec = pl.BlockSpec((rows, lanes), lambda i, at: (i, 0))
    outer_spec = pl.BlockSpec((outer_rows, columns), lambda i, at: (0, i))
    whole_inner = pl.BlockSpec((rows, lanes), lambda i, at: (at[0] * STEPS + i, 0))
    whole_outer = pl.BlockSpec((outer_rows, columns), lambda i, at: (at[0], i))
    height = 3 * rows + 3 * outer_rows * columns // lanes
    packed_spec = pl.BlockSpec((1, height, lanes), lambda i, at: (i, 0, 0))
    return inner_spec, outer_spec, whole_inner, whole_outer, packed_spec


def pack_kernel(at, first_in, second_in, weight_in, first_out, second_out, weight_out, packed):
    lanes = first_in.shape[1]
    inner, outer = sections(first_in.shape[0], first_out.shape[0], lanes, first_out.shape[1])
    moved = at[1] == 1

    def put(rows, value):
        packed[0, rows, :] = jnp.where(moved, value.astype(jnp.float32), 0.0).astype(packed.dtype)

    for rows, ref in zip(inner, (first_in, second_in, weight_in)):
        put(rows, ref[...])
    for parts, ref in zip(outer, (first_out, second_out, weight_out)):
        for p, rows in enumerate(parts):
            put(rows, ref[:, p * lanes : (p + 1) * lanes])


def pack(at, states, slot_in, slot_out):
    inner_spec, outer_spec, whole_inner, whole_outer, packed_spec = step_specs(states[0], states[2])
    return pl.pallas_call(
        pack_kernel,
        grid_spec=pltpu.PrefetchScalarGridSpec(
            num_scalar_prefetch=1,
            grid=(STEPS,),
            in_specs=[inner_spec, inner_spec, whole_inner, outer_spec, outer_spec, whole_outer],
            out_specs=packed_spec,
        ),
        out_shape=jax.ShapeDtypeStruct((STEPS,) + packed_spec.block_shape[1:], half_type),
        cost_estimate=pl.CostEstimate(flops=4 << 20, bytes_accessed=24 << 20, transcendentals=0),
    )(at, states[0], states[1], slot_in, states[2], states[3], slot_out)


def adam_kernel(
    at,
    packed,
    first_in,
    second_in,
    weight_in,
    first_out,
    second_out,
    weight_out,
    grad_in,
    grad_out,
    late_in,
    late_out,
    new_weight_in,
    new_first_in,
    new_second_in,
    new_weight_out,
    new_first_out,
    new_second_out,
):
    lanes = first_in.shape[1]
    inner, outer = sections(first_in.shape[0], first_out.shape[0], lanes, first_out.shape[1])
    moved = at[1] == 1
    one_column = at[2] == 1

    def placed(rows, stayed):
        came = packed[0, rows, :].astype(jnp.float32)
        came = came - jnp.where(one_column, stayed.astype(half_type).astype(jnp.float32), 0.0)
        return jnp.where(moved, came, stayed.astype(jnp.float32))

    new_weight_in[...], new_first_in[...], new_second_in[...] = adam_step(
        placed(inner[2], weight_in[...]),
        jnp.where(moved, late_in[...].astype(jnp.float32), grad_in[...]),
        placed(inner[0], first_in[...]),
        placed(inner[1], second_in[...]),
    )
    for p in range(len(outer[0])):
        part = slice(p * lanes, (p + 1) * lanes)
        new_weight_out[:, part], new_first_out[:, part], new_second_out[:, part] = adam_step(
            placed(outer[2][p], weight_out[:, part]),
            jnp.where(moved, late_out[:, part].astype(jnp.float32), grad_out[:, part]),
            placed(outer[0][p], first_out[:, part]),
            placed(outer[1][p], second_out[:, part]),
        )


def adam(at, packed, states, slot_in, slot_out, grad_in, grad_out, late_in, late_out):
    inner_spec, outer_spec, whole_inner, whole_outer, packed_spec = step_specs(states[0], states[2])
    inner_shape, outer_shape = states[0].shape, states[2].shape
    return pl.pallas_call(
        adam_kernel,
        grid_spec=pltpu.PrefetchScalarGridSpec(
            num_scalar_prefetch=1,
            grid=(STEPS,),
            in_specs=[packed_spec, inner_spec, inner_spec, whole_inner, outer_spec, outer_spec, whole_outer]
            + [inner_spec, outer_spec, inner_spec, outer_spec],
            out_specs=[inner_spec] * 3 + [outer_spec] * 3,
        ),
        out_shape=[
            jax.ShapeDtypeStruct(shape, dtype)
            for shape in (inner_shape, outer_shape)
            for dtype in (jnp.bfloat16, jnp.float32, jnp.float32)
        ],
        cost_estimate=pl.CostEstimate(flops=16 << 20, bytes_accessed=30 << 20, transcendentals=1 << 20),
        compiler_params=pltpu.CompilerParams(vmem_limit_bytes=52 * 1024 * 1024),
    )(at, packed, states[0], states[1], slot_in, states[2], states[3], slot_out, grad_in, grad_out, late_in, late_out)


def flip(value, axis):
    return lax.ppermute(value, axis, FLIP)


def tie(first, *others):
    return lax.optimization_barrier((first,) + others)[0]


def split_at(rows, share):
    return int(rows * share) // 16 * 16


def gather_groups(pieces, share, holds):
    cut = split_at(pieces[0].shape[0], share)
    near = [(flip(piece, "xl"), flip(piece, "z"), flip(piece, "c")) for piece in pieces]
    gathered = []
    last = None
    for piece, (from_x, from_z, from_c), hold in zip(pieces, near, holds):
        if last is not None:
            from_x, from_z = tie((from_x, from_z), last)
        if hold is not None:
            from_x, from_z = tie((from_x, from_z), hold)
        parts = []
        if cut:
            parts.append(flip(from_z[:cut], "xl"))
        if cut < piece.shape[0]:
            parts.append(flip(from_x[cut:], "z"))
        sides = flip(jnp.concatenate([from_x, from_z]), "c")
        diag = jnp.concatenate(parts)
        gathered.append([piece, from_x, from_z, from_c, sides, diag, flip(diag, "c")])
        last = diag
    return [jnp.concatenate(parts) for parts in gathered]


def reduce_start(array):
    rows = array.shape[0] // 8
    piece = lambda start, count=1: array[start * rows : (start + count) * rows]
    diag = (piece(6).astype(jnp.float32) + flip(piece(7), "c").astype(jnp.float32)).astype(half_type)
    sides = piece(1, 2).astype(jnp.float32) + flip(piece(4, 2), "c").astype(jnp.float32)
    own = piece(0).astype(jnp.float32) + flip(piece(3), "c").astype(jnp.float32)
    return own, sides, diag


def reduce_turn(sides, via_x, via_z):
    rows = sides.shape[0] // 2
    cut = via_x.shape[0]
    to_x, to_z = sides[:rows], sides[rows:]
    to_z = jnp.concatenate([to_z[:cut] + via_x.astype(jnp.float32), to_z[cut:]])
    to_x = jnp.concatenate([to_x[:cut], to_x[cut:] + via_z.astype(jnp.float32)])
    return to_x.astype(half_type), to_z.astype(half_type)


def exchange(values, distance):
    pairs = [(slot, slot ^ (distance * 8)) for slot in range(64)]
    return tuple(lax.ppermute(value, PARTS, pairs) for value in values)


def on_device(
    tokens,
    cotangent,
    expert_ids,
    gate_weights,
    holder,
    weight_in,
    weight_out,
    first_in,
    second_in,
    first_out,
    second_out,
):
    tok_rows, width = tokens.shape
    top_count = expert_ids.shape[1]
    groups = holder.shape[0]
    shards = 8
    routed = tok_rows * top_count
    capacity = 2 * routed // groups
    hidden = weight_out.shape[1]
    data_half = lax.axis_index("dp")
    columns = jnp.arange(groups, dtype=jnp.int32)
    my_expert = lax.axis_index("y") * 2 + lax.axis_index("xh")
    changed = holder != columns
    low = jnp.min(jnp.where(changed, columns, groups - 1))
    high = jnp.max(jnp.where(changed, columns, 0))
    case = jnp.clip((low ^ high) - 1, 0, 6)
    one_column = (low % 2) == (high % 2)
    moved = (my_expert == low) | (my_expert == high)
    slot_in = weight_in[0]
    slot_out = weight_out[0]
    states = (first_in[0], second_in[0], first_out[0], second_out[0])
    rows_in_half = first_in.shape[1]
    rows_out_half = first_out.shape[1]
    at = jnp.stack([data_half, moved, one_column]).astype(jnp.int32)

    flat_ids = expert_ids.reshape(routed)
    onehot = (flat_ids[:, None] == columns[None, :]).astype(jnp.int32)
    earlier = jnp.cumsum(onehot, axis=0) - onehot
    order_in = jnp.sum(earlier * onehot, axis=1)
    position = (flat_ids * capacity + order_in).reshape(tok_rows, top_count)
    places = jnp.arange(groups * capacity, dtype=jnp.int32)
    picks = position[:, :, None] == places[None, None, :]
    chosen = jnp.any(picks, axis=1).astype(jnp.bfloat16)
    gate_of = jnp.sum(jnp.where(picks, gate_weights[:, :, None], 0.0), axis=(0, 1))
    spread = (((0,), (0,)), ((), ()))
    group_inputs = lax.dot_general(chosen, tokens, spread, preferred_element_type=jnp.float32).astype(jnp.bfloat16)
    group_cots = (
        gate_of[:, None] * lax.dot_general(chosen, cotangent, spread, preferred_element_type=jnp.float32)
    ).astype(jnp.bfloat16)
    send = jnp.concatenate(
        [group_inputs.reshape(groups, capacity, width), group_cots.reshape(groups, capacity, width)], axis=1
    )
    at, send = lax.optimization_barrier((at, send))
    share = lax.psum_scatter(pack(at, states, slot_in, slot_out), "y", scatter_dimension=0, tiled=True)
    received = lax.all_to_all(send, GROUP, split_axis=0, concat_axis=0, tiled=True)
    rows_piece = received[:, :capacity].reshape(groups * capacity, width)
    cots_piece = received[:, capacity:].reshape(groups * capacity, width)
    rows_in, rows_cot = gather_groups((rows_piece, cots_piece), 0.5, (None, None))

    last_dims = (((1,), (1,)), ((), ()))
    first_dims = (((0,), (0,)), ((), ()))
    projected = jnp.dot(rows_in, slot_in, preferred_element_type=jnp.float32) * width ** (-0.5)
    projected, share = lax.optimization_barrier((projected, share))
    crossed = flip(share, "xh")
    gate_part = projected[:, :hidden]
    up_part = projected[:, hidden:]
    sigmoid = jax.nn.sigmoid(gate_part)
    activated = gate_part * sigmoid
    hidden_act = (activated * up_part).astype(jnp.bfloat16)
    outputs = (jnp.dot(hidden_act, slot_out, preferred_element_type=jnp.float32) * FF ** (-0.5)).astype(jnp.bfloat16)
    grad_hidden = lax.dot_general(rows_cot, slot_out, last_dims, preferred_element_type=jnp.float32) * FF ** (-0.5)
    slopes = sigmoid * (1.0 + gate_part * (1.0 - sigmoid))
    grad_gate = grad_hidden * up_part * slopes
    grad_up = grad_hidden * activated
    grad_pre = (jnp.concatenate([grad_gate, grad_up], axis=1) * width ** (-0.5)).astype(jnp.bfloat16)
    grad_rows = lax.dot_general(grad_pre, slot_in, last_dims, preferred_element_type=jnp.float32).astype(jnp.bfloat16)
    grad_in = lax.dot_general(rows_in, grad_pre, first_dims, preferred_element_type=jnp.float32)
    grad_out = lax.dot_general(hidden_act, rows_cot, first_dims, preferred_element_type=jnp.float32) * FF ** (-0.5)

    other_half = 1 - data_half
    away_in = lax.dynamic_slice_in_dim(grad_in, other_half * rows_in_half, rows_in_half, 0).astype(half_type)
    away_out = lax.dynamic_slice_in_dim(grad_out, other_half * rows_out_half, rows_out_half, 0).astype(half_type)
    kept_in = lax.dynamic_slice_in_dim(grad_in, data_half * rows_in_half, rows_in_half, 0)
    kept_out = lax.dynamic_slice_in_dim(grad_out, data_half * rows_out_half, rows_out_half, 0)
    away_in, away_out, share = lax.optimization_barrier((away_in, away_out, share))
    came_out = flip(away_out, "dp")
    came_in = flip(away_in, "dp")

    own_out, sides_out, diag_out = reduce_start(outputs)
    own_grad, sides_grad, diag_grad = reduce_start(grad_rows)
    diag_out, diag_grad, crossed = lax.optimization_barrier((diag_out, diag_grad, crossed))
    early = lax.all_gather(jnp.where(one_column, share, crossed), "y", axis=0, tiled=True)
    cut = diag_out.shape[0] // 2
    to_x, to_z = zip(
        *[
            reduce_turn(sides, flip(diag[:cut], "xl"), flip(diag[cut:], "z"))
            for sides, diag in ((sides_out, diag_out), (sides_grad, diag_grad))
        ]
    )
    came_in, came_out, to_x, to_z = lax.optimization_barrier((came_in, came_out, to_x, to_z))
    half_out = kept_out + came_out.astype(jnp.float32)
    half_in = kept_in + came_in.astype(jnp.float32)
    late_in, late_out = lax.switch(
        case,
        [functools.partial(exchange, distance=distance) for distance in DISTANCES],
        (half_in.astype(half_type), half_out.astype(half_type)),
    )
    out_sum, grad_sum = (
        own + flip(part_x, "xl").astype(jnp.float32) + flip(part_z, "z").astype(jnp.float32)
        for own, part_x, part_z in zip((own_out, own_grad), to_x, to_z)
    )
    back = jnp.concatenate(
        [
            out_sum.astype(half_type).reshape(groups, capacity, width),
            grad_sum.astype(half_type).reshape(groups, capacity, width),
        ],
        axis=1,
    )
    back = lax.all_to_all(back, GROUP, split_axis=0, concat_axis=0, tiled=True)
    new_weight_in, new_first_in, new_second_in, new_weight_out, new_first_out, new_second_out = adam(
        at, early, states, slot_in, slot_out, half_in, half_out, late_in, late_out
    )
    back, new_weight_in = lax.optimization_barrier((back, new_weight_in))
    back_out = back[:, :capacity].reshape(groups * capacity, width)
    back_grad = back[:, capacity:].reshape(groups * capacity, width)
    picked = picks.astype(jnp.bfloat16)
    layer_out = sum(
        gate_weights[:, k : k + 1] * jnp.dot(picked[:, k], back_out, preferred_element_type=jnp.float32)
        for k in range(top_count)
    ).astype(jnp.bfloat16)
    grad_tokens = jnp.dot(chosen, back_grad, preferred_element_type=jnp.float32).astype(jnp.bfloat16)

    return (
        layer_out,
        grad_tokens,
        new_weight_in[None],
        new_weight_out[None],
        new_first_in[None],
        new_second_in[None],
        new_first_out[None],
        new_second_out[None],
    )


def solution(mesh):
    fine = Mesh(mesh.devices.reshape(2, 4, 2, 2, 2, 2), ("dp",) + PARTS)
    rows = P(("dp",) + PARTS, None)
    slots = P(PARTS, None, None)
    halves = P(PARTS, "dp", None)
    return jax.shard_map(
        on_device,
        mesh=fine,
        in_specs=(rows, rows, rows, rows, P(), slots, slots, halves, halves, halves, halves),
        out_specs=(rows, rows, halves, halves, halves, halves, halves, halves),
        check_vma=False,
    )
```

```python
import functools

import jax
import jax.numpy as jnp
from jax import lax
from jax.experimental import pallas as pl
from jax.experimental.pallas import tpu as pltpu
from jax.sharding import Mesh, PartitionSpec as P

FF = 1024

beta_one = 0.9
beta_two = 0.95
learn_rate = 0.01
decay_rate = 0.1
epsilon = 1e-08

PARTS = ("y", "xh", "xl", "z", "c")
GROUP = ("y", "xh")
DISTANCES = range(1, 8)
FLIP = [(0, 1), (1, 0)]
half_type = jnp.bfloat16


def adam_step(weight, grad, first, second):
    first_new = beta_one * first + (1.0 - beta_one) * grad
    second_new = beta_two * second + (1.0 - beta_two) * grad * grad
    weight_new = (
        weight - learn_rate * (first_new / (jnp.sqrt(second_new) + epsilon) + decay_rate * weight)
    ).astype(jnp.bfloat16)
    return (weight_new, first_new, second_new)


STEPS = 8


def sections(inner_rows, outer_rows, lanes, outer_columns):
    parts = outer_columns // lanes
    inner = [slice(k * inner_rows, (k + 1) * inner_rows) for k in range(3)]
    start = 3 * inner_rows
    outer = [
        [
            slice(start + (k * parts + p) * outer_rows, start + (k * parts + p + 1) * outer_rows)
            for p in range(parts)
        ]
        for k in range(3)
    ]
    return inner, outer


def step_specs(inner, outer):
    rows, lanes = inner.shape[0] // STEPS, inner.shape[1]
    outer_rows, columns = outer.shape[0], outer.shape[1] // STEPS
    inner_spec = pl.BlockSpec((rows, lanes), lambda i, at: (i, 0))
    outer_spec = pl.BlockSpec((outer_rows, columns), lambda i, at: (0, i))
    whole_inner = pl.BlockSpec((rows, lanes), lambda i, at: (at[0] * STEPS + i, 0))
    whole_outer = pl.BlockSpec((outer_rows, columns), lambda i, at: (at[0], i))
    height = 3 * rows + 3 * outer_rows * columns // lanes
    packed_spec = pl.BlockSpec((1, height, lanes), lambda i, at: (i, 0, 0))
    return inner_spec, outer_spec, whole_inner, whole_outer, packed_spec


def pack_kernel(at, first_in, second_in, weight_in, first_out, second_out, weight_out, packed):
    lanes = first_in.shape[1]
    inner, outer = sections(first_in.shape[0], first_out.shape[0], lanes, first_out.shape[1])
    moved = at[1] == 1

    def put(rows, value):
        packed[0, rows, :] = jnp.where(moved, value.astype(jnp.float32), 0.0).astype(packed.dtype)

    for rows, ref in zip(inner, (first_in, second_in, weight_in)):
        put(rows, ref[...])
    for parts, ref in zip(outer, (first_out, second_out, weight_out)):
        for p, rows in enumerate(parts):
            put(rows, ref[:, p * lanes : (p + 1) * lanes])


def pack(at, states, slot_in, slot_out):
    inner_spec, outer_spec, whole_inner, whole_outer, packed_spec = step_specs(states[0], states[2])
    return pl.pallas_call(
        pack_kernel,
        grid_spec=pltpu.PrefetchScalarGridSpec(
            num_scalar_prefetch=1,
            grid=(STEPS,),
            in_specs=[inner_spec, inner_spec, whole_inner, outer_spec, outer_spec, whole_outer],
            out_specs=packed_spec,
        ),
        out_shape=jax.ShapeDtypeStruct((STEPS,) + packed_spec.block_shape[1:], half_type),
        cost_estimate=pl.CostEstimate(flops=4 << 20, bytes_accessed=24 << 20, transcendentals=0),
    )(at, states[0], states[1], slot_in, states[2], states[3], slot_out)


def adam_kernel(
    at,
    packed,
    first_in,
    second_in,
    weight_in,
    first_out,
    second_out,
    weight_out,
    grad_in,
    grad_out,
    late_in,
    late_out,
    new_weight_in,
    new_first_in,
    new_second_in,
    new_weight_out,
    new_first_out,
    new_second_out,
):
    lanes = first_in.shape[1]
    inner, outer = sections(first_in.shape[0], first_out.shape[0], lanes, first_out.shape[1])
    moved = at[1] == 1
    one_column = at[2] == 1

    def placed(rows, stayed):
        came = packed[0, rows, :].astype(jnp.float32)
        came = came - jnp.where(one_column, stayed.astype(half_type).astype(jnp.float32), 0.0)
        return jnp.where(moved, came, stayed.astype(jnp.float32))

    new_weight_in[...], new_first_in[...], new_second_in[...] = adam_step(
        placed(inner[2], weight_in[...]),
        jnp.where(moved, late_in[...].astype(jnp.float32), grad_in[...]),
        placed(inner[0], first_in[...]),
        placed(inner[1], second_in[...]),
    )
    for p in range(len(outer[0])):
        part = slice(p * lanes, (p + 1) * lanes)
        new_weight_out[:, part], new_first_out[:, part], new_second_out[:, part] = adam_step(
            placed(outer[2][p], weight_out[:, part]),
            jnp.where(moved, late_out[:, part].astype(jnp.float32), grad_out[:, part]),
            placed(outer[0][p], first_out[:, part]),
            placed(outer[1][p], second_out[:, part]),
        )


def adam(at, packed, states, slot_in, slot_out, grad_in, grad_out, late_in, late_out):
    inner_spec, outer_spec, whole_inner, whole_outer, packed_spec = step_specs(states[0], states[2])
    inner_shape, outer_shape = states[0].shape, states[2].shape
    return pl.pallas_call(
        adam_kernel,
        grid_spec=pltpu.PrefetchScalarGridSpec(
            num_scalar_prefetch=1,
            grid=(STEPS,),
            in_specs=[packed_spec, inner_spec, inner_spec, whole_inner, outer_spec, outer_spec, whole_outer]
            + [inner_spec, outer_spec, inner_spec, outer_spec],
            out_specs=[inner_spec] * 3 + [outer_spec] * 3,
        ),
        out_shape=[
            jax.ShapeDtypeStruct(shape, dtype)
            for shape in (inner_shape, outer_shape)
            for dtype in (jnp.bfloat16, jnp.float32, jnp.float32)
        ],
        cost_estimate=pl.CostEstimate(flops=16 << 20, bytes_accessed=30 << 20, transcendentals=1 << 20),
        compiler_params=pltpu.CompilerParams(vmem_limit_bytes=52 * 1024 * 1024),
    )(at, packed, states[0], states[1], slot_in, states[2], states[3], slot_out, grad_in, grad_out, late_in, late_out)


def flip(value, axis):
    return lax.ppermute(value, axis, FLIP)


def tie(first, *others):
    return lax.optimization_barrier((first,) + others)[0]


def split_at(rows, share):
    return int(rows * share) // 16 * 16


def gather_groups(pieces, share, holds):
    cut = split_at(pieces[0].shape[0], share)
    near = [(flip(piece, "xl"), flip(piece, "z"), flip(piece, "c")) for piece in pieces]
    gathered = []
    last = None
    for piece, (from_x, from_z, from_c), hold in zip(pieces, near, holds):
        if last is not None:
            from_x, from_z = tie((from_x, from_z), last)
        if hold is not None:
            from_x, from_z = tie((from_x, from_z), hold)
        parts = []
        if cut:
            parts.append(flip(from_z[:cut], "xl"))
        if cut < piece.shape[0]:
            parts.append(flip(from_x[cut:], "z"))
        sides = flip(jnp.concatenate([from_x, from_z]), "c")
        diag = jnp.concatenate(parts)
        gathered.append([piece, from_x, from_z, from_c, sides, diag, flip(diag, "c")])
        last = diag
    return [jnp.concatenate(parts) for parts in gathered]


def reduce_start(array):
    rows = array.shape[0] // 8
    piece = lambda start, count=1: array[start * rows : (start + count) * rows]
    diag = (piece(6).astype(jnp.float32) + flip(piece(7), "c").astype(jnp.float32)).astype(half_type)
    sides = piece(1, 2).astype(jnp.float32) + flip(piece(4, 2), "c").astype(jnp.float32)
    own = piece(0).astype(jnp.float32) + flip(piece(3), "c").astype(jnp.float32)
    return own, sides, diag


def reduce_turn(sides, via_x, via_z):
    rows = sides.shape[0] // 2
    cut = via_x.shape[0]
    to_x, to_z = sides[:rows], sides[rows:]
    to_z = jnp.concatenate([to_z[:cut] + via_x.astype(jnp.float32), to_z[cut:]])
    to_x = jnp.concatenate([to_x[:cut], to_x[cut:] + via_z.astype(jnp.float32)])
    return to_x.astype(half_type), to_z.astype(half_type)


def exchange(values, distance):
    pairs = [(slot, slot ^ (distance * 8)) for slot in range(64)]
    return tuple(lax.ppermute(value, PARTS, pairs) for value in values)


def on_device(
    tokens,
    cotangent,
    expert_ids,
    gate_weights,
    holder,
    weight_in,
    weight_out,
    first_in,
    second_in,
    first_out,
    second_out,
):
    tok_rows, width = tokens.shape
    top_count = expert_ids.shape[1]
    groups = holder.shape[0]
    shards = 8
    routed = tok_rows * top_count
    capacity = 2 * routed // groups
    hidden = weight_out.shape[1]
    data_half = lax.axis_index("dp")
    columns = jnp.arange(groups, dtype=jnp.int32)
    my_expert = lax.axis_index("y") * 2 + lax.axis_index("xh")
    changed = holder != columns
    low = jnp.min(jnp.where(changed, columns, groups - 1))
    high = jnp.max(jnp.where(changed, columns, 0))
    case = jnp.clip((low ^ high) - 1, 0, 6)
    one_column = (low % 2) == (high % 2)
    moved = (my_expert == low) | (my_expert == high)
    slot_in = weight_in[0]
    slot_out = weight_out[0]
    states = (first_in[0], second_in[0], first_out[0], second_out[0])
    rows_in_half = first_in.shape[1]
    rows_out_half = first_out.shape[1]
    at = jnp.stack([data_half, moved, one_column]).astype(jnp.int32)

    flat_ids = expert_ids.reshape(routed)
    onehot = (flat_ids[:, None] == columns[None, :]).astype(jnp.int32)
    earlier = jnp.cumsum(onehot, axis=0) - onehot
    order_in = jnp.sum(earlier * onehot, axis=1)
    position = (flat_ids * capacity + order_in).reshape(tok_rows, top_count)
    places = jnp.arange(groups * capacity, dtype=jnp.int32)
    picks = position[:, :, None] == places[None, None, :]
    chosen = jnp.any(picks, axis=1).astype(jnp.bfloat16)
    gate_of = jnp.sum(jnp.where(picks, gate_weights[:, :, None], 0.0), axis=(0, 1))
    spread = (((0,), (0,)), ((), ()))
    group_inputs = lax.dot_general(chosen, tokens, spread, preferred_element_type=jnp.float32).astype(jnp.bfloat16)
    group_cots = (
        gate_of[:, None] * lax.dot_general(chosen, cotangent, spread, preferred_element_type=jnp.float32)
    ).astype(jnp.bfloat16)
    send = jnp.concatenate(
        [group_inputs.reshape(groups, capacity, width), group_cots.reshape(groups, capacity, width)], axis=1
    )
    at, send = lax.optimization_barrier((at, send))
    share = lax.psum_scatter(pack(at, states, slot_in, slot_out), "y", scatter_dimension=0, tiled=True)
    received = lax.all_to_all(send, GROUP, split_axis=0, concat_axis=0, tiled=True)
    rows_piece = received[:, :capacity].reshape(groups * capacity, width)
    cots_piece = received[:, capacity:].reshape(groups * capacity, width)
    rows_in, rows_cot = gather_groups((rows_piece, cots_piece), 0.5, (None, None))

    last_dims = (((1,), (1,)), ((), ()))
    first_dims = (((0,), (0,)), ((), ()))
    projected = jnp.dot(rows_in, slot_in, preferred_element_type=jnp.float32) * width ** (-0.5)
    projected, share = lax.optimization_barrier((projected, share))
    crossed = flip(share, "xh")
    gate_part = projected[:, :hidden]
    up_part = projected[:, hidden:]
    sigmoid = jax.nn.sigmoid(gate_part)
    activated = gate_part * sigmoid
    hidden_act = (activated * up_part).astype(jnp.bfloat16)
    outputs = (jnp.dot(hidden_act, slot_out, preferred_element_type=jnp.float32) * FF ** (-0.5)).astype(jnp.bfloat16)
    grad_hidden = lax.dot_general(rows_cot, slot_out, last_dims, preferred_element_type=jnp.float32) * FF ** (-0.5)
    slopes = sigmoid * (1.0 + gate_part * (1.0 - sigmoid))
    grad_gate = grad_hidden * up_part * slopes
    grad_up = grad_hidden * activated
    grad_pre = (jnp.concatenate([grad_gate, grad_up], axis=1) * width ** (-0.5)).astype(jnp.bfloat16)
    grad_rows = lax.dot_general(grad_pre, slot_in, last_dims, preferred_element_type=jnp.float32).astype(jnp.bfloat16)
    grad_in = lax.dot_general(rows_in, grad_pre, first_dims, preferred_element_type=jnp.float32)
    grad_out = lax.dot_general(hidden_act, rows_cot, first_dims, preferred_element_type=jnp.float32) * FF ** (-0.5)

    other_half = 1 - data_half
    away_in = lax.dynamic_slice_in_dim(grad_in, other_half * rows_in_half, rows_in_half, 0).astype(half_type)
    away_out = lax.dynamic_slice_in_dim(grad_out, other_half * rows_out_half, rows_out_half, 0).astype(half_type)
    kept_in = lax.dynamic_slice_in_dim(grad_in, data_half * rows_in_half, rows_in_half, 0)
    kept_out = lax.dynamic_slice_in_dim(grad_out, data_half * rows_out_half, rows_out_half, 0)
    away_in, away_out, share = lax.optimization_barrier((away_in, away_out, share))
    came_out = flip(away_out, "dp")
    came_in = flip(away_in, "dp")

    own_out, sides_out, diag_out = reduce_start(outputs)
    own_grad, sides_grad, diag_grad = reduce_start(grad_rows)
    diag_out, diag_grad, crossed = lax.optimization_barrier((diag_out, diag_grad, crossed))
    early = lax.all_gather(jnp.where(one_column, share, crossed), "y", axis=0, tiled=True)
    cut = diag_out.shape[0] // 2
    to_x, to_z = zip(
        *[
            reduce_turn(sides, flip(diag[:cut], "xl"), flip(diag[cut:], "z"))
            for sides, diag in ((sides_out, diag_out), (sides_grad, diag_grad))
        ]
    )
    to_x, to_z = jnp.stack(to_x), jnp.stack(to_z)
    came_in, came_out, to_x, to_z = lax.optimization_barrier((came_in, came_out, to_x, to_z))
    half_out = kept_out + came_out.astype(jnp.float32)
    half_in = kept_in + came_in.astype(jnp.float32)
    late_in, late_out = lax.switch(
        case,
        [functools.partial(exchange, distance=distance) for distance in DISTANCES],
        (half_in.astype(half_type), half_out.astype(half_type)),
    )
    last_x = flip(to_x, "xl")
    last_z = flip(to_z, "z")
    last_x, last_z, late_in, late_out = lax.optimization_barrier((last_x, last_z, late_in, late_out))
    out_sum, grad_sum = (
        own + part_x.astype(jnp.float32) + part_z.astype(jnp.float32)
        for own, part_x, part_z in zip((own_out, own_grad), last_x, last_z)
    )
    back = jnp.concatenate(
        [
            out_sum.astype(half_type).reshape(groups, capacity, width),
            grad_sum.astype(half_type).reshape(groups, capacity, width),
        ],
        axis=1,
    )
    back = lax.all_to_all(back, GROUP, split_axis=0, concat_axis=0, tiled=True)
    new_weight_in, new_first_in, new_second_in, new_weight_out, new_first_out, new_second_out = adam(
        at, early, states, slot_in, slot_out, half_in, half_out, late_in, late_out
    )
    back, new_weight_in = lax.optimization_barrier((back, new_weight_in))
    back_out = back[:, :capacity].reshape(groups * capacity, width)
    back_grad = back[:, capacity:].reshape(groups * capacity, width)
    picked = picks.astype(jnp.bfloat16)
    layer_out = sum(
        gate_weights[:, k : k + 1] * jnp.dot(picked[:, k], back_out, preferred_element_type=jnp.float32)
        for k in range(top_count)
    ).astype(jnp.bfloat16)
    grad_tokens = jnp.dot(chosen, back_grad, preferred_element_type=jnp.float32).astype(jnp.bfloat16)

    return (
        layer_out,
        grad_tokens,
        new_weight_in[None],
        new_weight_out[None],
        new_first_in[None],
        new_second_in[None],
        new_first_out[None],
        new_second_out[None],
    )


def solution(mesh):
    fine = Mesh(mesh.devices.reshape(2, 4, 2, 2, 2, 2), ("dp",) + PARTS)
    rows = P(("dp",) + PARTS, None)
    slots = P(PARTS, None, None)
    halves = P(PARTS, "dp", None)
    return jax.shard_map(
        on_device,
        mesh=fine,
        in_specs=(rows, rows, rows, rows, P(), slots, slots, halves, halves, halves, halves),
        out_specs=(rows, rows, halves, halves, halves, halves, halves, halves),
        check_vma=False,
    )
```
